32 devices in a mesh: section: 2 (over y), dp: 4 (over z), tensor: 4 (over x, core).
Axes of the slice: x: 2, y: 2, z: 4, core: 2. Of those that a mesh axis runs over, the one named last changes fastest.
Arguments:
- layer_input: bfloat16 [2, 2, 256, 8192], P('section', None, 'tensor', 'dp'), may hold values from -64 to 64
- ready_grad: bfloat16 [2, 256, 8192], P('section', 'tensor', 'dp'), may hold values from -6 to 6
- late_grad: bfloat16 [256, 8192], P('tensor', 'dp'), may hold values from -6 to 6
- norm_gain: float32 [2, 8192], P('section', 'dp'), may hold values from 0.25 to 4.5
- norm_bias: float32 [2, 8192], P('section', 'dp'), may hold values from -3 to 3
- up_weight: bfloat16 [2, 8192, 16384], P('section', 'dp', 'tensor'), may hold values from -0.0625 to 0.0625
- down_weight: bfloat16 [2, 16384, 8192], P('section', 'tensor', 'dp'), may hold values from -0.046875 to 0.046875
Outputs:
- input_grad: bfloat16 [2, 2, 256, 8192], P('section', None, 'tensor', 'dp')
- up_grad: bfloat16 [2, 8192, 16384], P('section', 'dp', 'tensor')
- down_grad: bfloat16 [2, 16384, 8192], P('section', 'tensor', 'dp')
- gain_grad: float32 [2, 8192], P('section', 'dp')
- bias_grad: float32 [2, 8192], P('section', 'dp')
The draws below stay inside these ranges and needn't reach their ends.
All inputs are finite; a program needn't handle non-finite values.
Results may differ from the reference program's by a relative error of at most 0.03.
Values may be sent and summed in bfloat16 or wider, within the bound.
A program may use at most 192 MiB of HBM per device.

```python
import math
import jax
import jax.numpy as jnp
from jax import lax

MODEL_WIDTH = 8192
FF = 16384
TOKENS = 256
N_DP = 4


def draw_layer_input(key, part):
    key_rows, key_cols, key_base = jax.random.split(key, 3)
    row_scale = jnp.exp(jax.random.uniform(key_rows, (2, 2, TOKENS, 1), jnp.float32, 0.0, math.log(10.0)))
    col_scale = jnp.exp(jax.random.uniform(key_cols, (2, 1, 1, MODEL_WIDTH), jnp.float32, 0.0, math.log(10.0)))
    ramp = 1.0 + 2.0 * jnp.arange(MODEL_WIDTH, dtype=jnp.float32) / MODEL_WIDTH
    base = jnp.clip(jax.random.normal(key_base, (2, 2, TOKENS, MODEL_WIDTH), jnp.float32), -4.0, 4.0)
    return (0.02 * base * row_scale * col_scale * ramp).astype(jnp.bfloat16)


def draw_norm_gain(key, part):
    key_jitter = jax.random.fold_in(key, 7)
    position = jnp.arange(MODEL_WIDTH, dtype=jnp.float32) / MODEL_WIDTH
    jitter = jax.random.uniform(key_jitter, (2, MODEL_WIDTH), jnp.float32, 0.8, 1.2)
    ramp = 0.5 * jnp.exp(position * math.log(4.0))
    return (ramp * jitter).astype(jnp.float32)


def with_spikes(drawn, stream_key, source, target, parts, factor):
    def block_of(axis_at):
        return (jnp.arange(drawn.shape[axis_at]) // (drawn.shape[axis_at] // parts)).reshape((-1,) + (1,) * (drawn.ndim - 1 - axis_at))

    one_side = jax.random.permutation(stream_key, parts)[block_of(target)]
    second = (block_of(target) + parts // 2) % parts
    return jnp.where((block_of(source) == one_side) | (block_of(source) == second), factor * drawn, drawn)


def levels(key, extent, cuts, smallest, high):
    level = 1.0
    for dim, blocks in cuts:
        draws = jax.random.uniform(jax.random.fold_in(jax.random.fold_in(key, 6), dim), (blocks,), jnp.float32, smallest / len(cuts), high / len(cuts))
        level = level * jnp.repeat(jnp.exp(draws), extent[dim] // blocks).reshape((-1,) + (1,) * (len(extent) - 1 - dim))
    return level


def scatter_about(rng, shape, spread, bound, cuts=(), kind=jnp.bfloat16):
    array = jax.random.normal(rng, shape, jnp.float32) * spread
    if len(cuts) > 0:
        array = levels(rng, shape, cuts, -0.22, 0.18) * array
    return jnp.clip(array, min=-bound, max=bound).astype(kind)


def heavy_noise(key, dims, deviation, reach, cuts, heavy, kind=jnp.bfloat16):
    array = deviation * jax.random.normal(key, dims, jnp.float32)
    if cuts:
        array = array * levels(key, dims, cuts, -0.22, 0.18)
    return jnp.clip(with_spikes(array, jax.random.fold_in(key, 3), *heavy), -reach, reach).astype(kind)


def setup_inputs(seed: int = 0) -> dict:
    streams_of = jax.random.split(jax.random.key(seed), 8)
    layer_input = draw_layer_input(jax.random.fold_in(streams_of[7], 71), 0)
    ready_grad = heavy_noise(streams_of[1], (2, TOKENS, MODEL_WIDTH), 1.0, 6.0, ((0, 2), (1, 4), (2, 4)), (2, 1, 4, 2.0))
    late_grad = heavy_noise(streams_of[2], (TOKENS, MODEL_WIDTH), 1.0, 6.0, ((0, 4), (1, 4)), (1, 0, 4, 2.0))
    norm_gain = draw_norm_gain(jax.random.fold_in(streams_of[7], 71), 0)
    norm_bias = scatter_about(streams_of[4], (2, MODEL_WIDTH), 0.5, 3.0, ((0, 2), (1, 4)), jnp.float32)
    up_weight = scatter_about(streams_of[5], (2, MODEL_WIDTH, FF), MODEL_WIDTH ** -0.5, 0.0625, ((0, 2), (1, 4), (2, 4)))
    down_weight = scatter_about(streams_of[6], (2, FF, MODEL_WIDTH), FF ** -0.5, 0.046875, ((0, 2), (1, 4), (2, 4)))
    return dict(layer_input=layer_input, ready_grad=ready_grad, late_grad=late_grad, norm_gain=norm_gain, norm_bias=norm_bias, up_weight=up_weight, down_weight=down_weight)


epsilon = 1e-05
inv_root_two = 0.7071067811865476
inv_root_two_pi = 0.3989422804014327

def gelu_value(values):
    return 0.5 * values * (1.0 + lax.erf(values * inv_root_two))

def gelu_slope(values):
    return 0.5 * (1.0 + lax.erf(values * inv_root_two)) + values * jnp.exp(-0.5 * values * values) * inv_root_two_pi

def block_sum(left_rows, right_cols, blocks):
    width = left_rows.shape[1] // blocks
    total = jnp.zeros((left_rows.shape[0], right_cols.shape[1]), jnp.float32)
    for index in range(blocks):
        partial_value = jnp.dot(left_rows[:, index * width:(index + 1) * width], right_cols[index * width:(index + 1) * width, :], preferred_element_type=jnp.float32)
        rounded = lax.optimization_barrier(partial_value.astype(jnp.bfloat16))
        total = total + rounded.astype(jnp.float32)
    return total

def section_pass(inputs_bf, incoming_gradient, scale_gain, shift_bias, weight_up, weight_down):
    inputs_float = inputs_bf.astype(jnp.float32)
    row_mean = lax.optimization_barrier(jnp.sum(inputs_float, axis=1, keepdims=True)) / MODEL_WIDTH
    variance = lax.optimization_barrier(jnp.sum(inputs_float * inputs_float, axis=1, keepdims=True)) / MODEL_WIDTH - row_mean * row_mean
    inverse_deviation = lax.rsqrt(variance + epsilon)
    centered_input = (inputs_float - row_mean) * inverse_deviation
    normalized = (centered_input * scale_gain + shift_bias).astype(jnp.bfloat16)
    pre = block_sum(normalized, weight_up, N_DP)
    act = gelu_value(pre).astype(jnp.bfloat16)
    down_term = jnp.dot(act.T, incoming_gradient, preferred_element_type=jnp.float32)
    act_grad = block_sum(incoming_gradient, weight_down.T, N_DP)
    pre_grad = (act_grad * gelu_slope(pre)).astype(jnp.bfloat16)
    up_term = jnp.dot(normalized.T, pre_grad, preferred_element_type=jnp.float32)
    normalized_gradient = jnp.dot(pre_grad, weight_up.T, preferred_element_type=jnp.float32)
    gain_product = lax.optimization_barrier(jnp.sum(normalized_gradient * centered_input, axis=0))
    bias_term = lax.optimization_barrier(jnp.sum(normalized_gradient, axis=0))
    centered_gradient = normalized_gradient * scale_gain
    first_section = lax.optimization_barrier(jnp.sum(centered_gradient, axis=1, keepdims=True)) / MODEL_WIDTH
    second_section = lax.optimization_barrier(jnp.sum(centered_gradient * centered_input, axis=1, keepdims=True)) / MODEL_WIDTH
    final_output = incoming_gradient.astype(jnp.float32) + inverse_deviation * (centered_gradient - first_section - centered_input * second_section)
    return (final_output.astype(jnp.bfloat16), down_term, up_term, gain_product, bias_term)

def reference(layer_input, ready_grad, late_grad, norm_gain, norm_bias, up_weight, down_weight):
    scale = 1.0 / math.sqrt(2 * TOKENS)

    def run(section_id, micro, incoming_gradient):
        return section_pass(layer_input[section_id, micro], incoming_gradient, norm_gain[section_id], norm_bias[section_id], up_weight[section_id], down_weight[section_id])
    late_first = run(1, 0, ready_grad[1])
    late_second = run(1, 1, late_grad)
    early_first = run(0, 0, ready_grad[0])
    early_second = run(0, 1, late_first[0])
    passes = [(early_first, early_second), (late_first, late_second)]
    input_list, up_list, down_list, gain_list, bias_list = ([], [], [], [], [])
    for pair in passes:
        input_list.append(jnp.stack([pair[0][0], pair[1][0]]))
        down_list.append(((pair[0][1] + pair[1][1]) * scale).astype(jnp.bfloat16))
        up_list.append(((pair[0][2] + pair[1][2]) * scale).astype(jnp.bfloat16))
        gain_list.append((pair[0][3] + pair[1][3]) * scale)
        bias_list.append((pair[0][4] + pair[1][4]) * scale)
    return (jnp.stack(input_list), jnp.stack(up_list), jnp.stack(down_list), jnp.stack(gain_list), jnp.stack(bias_list))
```

```python
import functools
import math

import jax
import jax.numpy as jnp
from jax import lax
from jax.experimental import pallas as pl
from jax.experimental.pallas import tpu as pltpu
from jax.sharding import PartitionSpec as P

MODEL_WIDTH = 8192
MESH = pl.DeviceIdType.MESH

epsilon = 1e-05
inv_root_two = 0.7071067811865476
inv_root_two_pi = 0.3989422804014327


def relay_kernel(kind, n, *refs):
    has_pre, has_act = kind != "grad", kind != "value"
    it = iter(refs)
    norm_ref = next(it) if has_pre else None
    inc_ref = next(it) if has_act else None
    slope_ref = next(it) if kind == "grad" else None
    up_hbm = next(it)
    down_hbm = next(it) if has_act else None
    act_ref = next(it) if has_pre else None
    slope_out = next(it) if kind == "value" else None
    pg_ref, ng_ref = (next(it), next(it)) if has_act else (None, None)
    up_v, up_sem = next(it), next(it)
    down_v, down_sem = (next(it), next(it)) if has_act else (None, None)
    own, right_sum, left_sum = next(it), next(it), next(it)
    send_r, recv_r, send_l, recv_l = next(it), next(it), next(it), next(it)
    acc = next(it) if has_act else None

    chunks, width = up_v.shape[0], up_v.shape[2]
    streams = own.shape[0]
    me = lax.axis_index("dp")
    not_first, not_last = me > 0, me < n - 1

    def up_copy(c):
        cols = pl.ds(pl.multiple_of(c * width, width), width)
        return pltpu.make_async_copy(up_hbm.at[:, cols], up_v.at[c], up_sem.at[c])

    def down_copy(c):
        slots = down_v.shape[0]
        rows = pl.ds(pl.multiple_of(c * width, width), width)
        slot = lax.rem(c, slots)
        return pltpu.make_async_copy(down_hbm.at[rows, :], down_v.at[slot], down_sem.at[slot])

    def right_copy(s, c):
        return pltpu.make_async_remote_copy(
            right_sum.at[s, c], right_sum.at[s, c], send_r.at[s, c], recv_r.at[s, c],
            device_id={"dp": jnp.minimum(me + 1, n - 1)}, device_id_type=MESH)

    def left_copy(s, c):
        return pltpu.make_async_remote_copy(
            left_sum.at[s, c], left_sum.at[s, c], send_l.at[s, c], recv_l.at[s, c],
            device_id={"dp": jnp.maximum(me - 1, 0)}, device_id_type=MESH)

    if has_act:
        for c in range(min(down_v.shape[0], chunks)):
            down_copy(c).start()
    lax.fori_loop(0, chunks, lambda c, _: (up_copy(c).start(), 0)[1], 0)

    barrier = pltpu.get_barrier_semaphore()

    @pl.when(not_first)
    def _():
        pl.semaphore_signal(barrier, inc=1, device_id={"dp": me - 1}, device_id_type=MESH)

    @pl.when(not_last)
    def _():
        pl.semaphore_signal(barrier, inc=1, device_id={"dp": me + 1}, device_id_type=MESH)

    pl.semaphore_wait(barrier, jnp.where(not_first, 1, 0) + jnp.where(not_last, 1, 0))

    if has_act:
        acc[...] = jnp.zeros_like(acc)

    def forward(c, arrives, leaves, buf, copy):
        for s in range(streams):
            @pl.when(arrives)
            def _():
                copy(s, c).wait_recv()
                buf[s, c] = (buf[s, c].astype(jnp.float32) + own[s, c].astype(jnp.float32)).astype(jnp.bfloat16)

            @pl.when(jnp.logical_not(arrives))
            def _():
                buf[s, c] = own[s, c]

            @pl.when(leaves)
            def _():
                copy(s, c).start()

    def whole(s, c):
        return (right_sum[s, c].astype(jnp.float32) + left_sum[s, c].astype(jnp.float32)
                - own[s, c].astype(jnp.float32))

    def step(t, carry):
        @pl.when(t < chunks)
        def _():
            up_copy(t).wait()
            if has_pre:
                own[0, t] = jnp.dot(norm_ref[...], up_v[t], preferred_element_type=jnp.float32).astype(jnp.bfloat16)
            if has_act:
                down_copy(t).wait()
                own[streams - 1, t] = lax.dot_general(
                    inc_ref[...], down_v[lax.rem(t, down_v.shape[0])], (((1,), (1,)), ((), ())),
                    preferred_element_type=jnp.float32).astype(jnp.bfloat16)

                @pl.when(t + down_v.shape[0] < chunks)
                def _():
                    down_copy(t + down_v.shape[0]).start()

        cr = t - 2 * me
        @pl.when(jnp.logical_and(cr >= 0, cr < chunks))
        def _():
            forward(cr, not_first, not_last, right_sum, right_copy)

        cl = t - 2 * (n - 1 - me)
        @pl.when(jnp.logical_and(cl >= 0, cl < chunks))
        def _():
            forward(cl, not_last, not_first, left_sum, left_copy)

        c = t - 2 * (n - 1)
        @pl.when(c >= 0)
        def _():
            cols = pl.ds(pl.multiple_of(c * width, width), width)
            if has_pre:
                pre = whole(0, c)
                cdf = 0.5 * (1.0 + lax.erf(pre * inv_root_two))
                slope = cdf + pre * jnp.exp(-0.5 * pre * pre) * inv_root_two_pi
                act_ref[:, cols] = (pre * cdf).astype(jnp.bfloat16)
                if kind == "value":
                    slope_out[:, cols] = slope
            else:
                slope = slope_ref[:, cols]
            if has_act:
                grad = (whole(streams - 1, c) * slope).astype(jnp.bfloat16)
                pg_ref[:, cols] = grad
                acc[...] += lax.dot_general(grad, up_v[c], (((1,), (1,)), ((), ())),
                                            preferred_element_type=jnp.float32)
        return carry

    lax.fori_loop(0, chunks + 2 * (n - 1), step, 0)

    if has_act:
        ng_ref[...] = acc[...].astype(jnp.bfloat16)

    def drain(c, carry):
        for s in range(streams):
            @pl.when(not_last)
            def _():
                right_copy(s, c).wait_send()

            @pl.when(not_first)
            def _():
                left_copy(s, c).wait_send()
        return carry

    lax.fori_loop(0, chunks, drain, 0)


def relay(kind, collective_id, lhs, up, down=None):
    n = lax.axis_size("dp")
    tokens = lhs[0].shape[0]
    features, hidden = up.shape
    width = 256
    chunks = hidden // width
    has_pre, has_act = kind != "grad", kind != "value"
    streams = 2 if kind == "both" else 1
    vmem = pl.BlockSpec(memory_space=pltpu.VMEM)
    hbm = pl.BlockSpec(memory_space=pl.ANY)
    wide = jax.ShapeDtypeStruct((tokens, hidden), jnp.bfloat16)
    outs = []
    if has_pre:
        outs.append(wide)
    if kind == "value":
        outs.append(jax.ShapeDtypeStruct((tokens, hidden), jnp.float32))
    if has_act:
        outs += [wide, jax.ShapeDtypeStruct((tokens, features), jnp.bfloat16)]
    sems = pltpu.SemaphoreType.DMA
    scratch = [pltpu.VMEM((chunks, features, width), jnp.bfloat16), sems((chunks,))]
    if has_act:
        scratch += [pltpu.VMEM((4, width, features), jnp.bfloat16), sems((4,))]
    scratch += [pltpu.VMEM((streams, chunks, tokens, width), jnp.bfloat16)] * 3
    scratch += [sems((streams, chunks))] * 4
    if has_act:
        scratch.append(pltpu.VMEM((tokens, features), jnp.float32))
    weights = [up] + ([down] if has_act else [])
    products = (1 if has_pre else 0) + (2 if has_act else 0)
    return pl.pallas_call(
        functools.partial(relay_kernel, kind, n),
        out_shape=outs,
        in_specs=[vmem] * len(lhs) + [hbm] * len(weights),
        out_specs=[vmem] * len(outs),
        scratch_shapes=scratch,
        compiler_params=pltpu.CompilerParams(
            collective_id=collective_id, has_side_effects=True,
            vmem_limit_bytes=52 * 1024 * 1024),
        cost_estimate=pl.CostEstimate(
            flops=2 * tokens * features * hidden * products,
            bytes_accessed=streams * 160 * 1024 * 1024, transcendentals=0),
        name="relay_" + kind,
    )(*lhs, *weights)


def finish(partial_gradient, centered_input, inverse_deviation, scale_gain, local_rows):
    normalized_gradient = lax.psum_scatter(
        partial_gradient, "tensor", scatter_dimension=0, tiled=True).astype(jnp.float32)
    gain_product = jnp.sum(normalized_gradient * centered_input, axis=0)
    bias_term = jnp.sum(normalized_gradient, axis=0)
    centered_gradient = normalized_gradient * scale_gain
    centered_total, centered_cross = lax.psum(
        (
            jnp.sum(centered_gradient, axis=1, keepdims=True),
            jnp.sum(centered_gradient * centered_input, axis=1, keepdims=True),
        ),
        "dp",
    )
    final_output = local_rows.astype(jnp.float32) + inverse_deviation * (
        centered_gradient
        - centered_total / MODEL_WIDTH
        - centered_input * (centered_cross / MODEL_WIDTH)
    )
    return final_output.astype(jnp.bfloat16), gain_product, bias_term


def gather_rows(block):
    return lax.all_gather(block, "tensor", axis=0, tiled=True)


def body(layer_input, ready_grad, late_grad, norm_gain, norm_bias, up_weight, down_weight):
    early = lax.axis_index("section") == 0
    scale_gain = norm_gain[0]
    shift_bias = norm_bias[0]
    weight_up = up_weight[0]
    weight_down = down_weight[0]
    ready_whole = gather_rows(ready_grad[0])
    inputs_float = layer_input[0].astype(jnp.float32)
    row_total, row_squares = lax.psum(
        (
            jnp.sum(inputs_float, axis=2, keepdims=True),
            jnp.sum(inputs_float * inputs_float, axis=2, keepdims=True),
        ),
        "dp",
    )
    row_mean = row_total / MODEL_WIDTH
    variance = row_squares / MODEL_WIDTH - row_mean * row_mean
    inverse_deviation = lax.rsqrt(variance + epsilon)
    centered_input = (inputs_float - row_mean) * inverse_deviation
    normalized = (centered_input * scale_gain + shift_bias).astype(jnp.bfloat16)
    normed_first = gather_rows(normalized[0])
    act_first, pre_grad_first, partial_first = relay(
        "both", 1, [normed_first, ready_whole], weight_up, weight_down)
    normed_second = gather_rows(normalized[1])
    act_second, slope_second = relay("value", 2, [normed_second], weight_up)
    first_out, first_gain, first_bias = finish(
        partial_first, centered_input[0], inverse_deviation[0], scale_gain, ready_grad[0])

    arrived = lax.ppermute(first_out, "section", [(1, 0)])
    second_rows = jnp.where(early, arrived, late_grad)
    second_incoming = gather_rows(second_rows)
    pre_grad_second, partial_second = relay(
        "grad", 3, [second_incoming, slope_second], weight_up, weight_down)
    second_out, second_gain, second_bias = finish(
        partial_second, centered_input[1], inverse_deviation[1], scale_gain, second_rows)

    scale = 1.0 / math.sqrt(2 * second_incoming.shape[0])

    def weight_grad(left, right):
        return (lax.dot_general(
            jnp.concatenate(left), jnp.concatenate(right), (((0,), (0,)), ((), ())),
            preferred_element_type=jnp.float32) * scale).astype(jnp.bfloat16)

    down_part = weight_grad([act_first, act_second], [ready_whole, second_incoming])
    up_part = weight_grad([normed_first, normed_second], [pre_grad_first, pre_grad_second])
    gain_sum, bias_sum = lax.psum((first_gain + second_gain, first_bias + second_bias), "tensor")
    results = jnp.stack([first_out, second_out])
    return (
        results[None],
        up_part[None],
        down_part[None],
        (gain_sum * scale)[None],
        (bias_sum * scale)[None],
    )


def solution(mesh):
    in_specs = (
        P("section", None, "tensor", "dp"),
        P("section", "tensor", "dp"),
        P("tensor", "dp"),
        P("section", "dp"),
        P("section", "dp"),
        P("section", "dp", "tensor"),
        P("section", "tensor", "dp"),
    )
    out_specs = (
        P("section", None, "tensor", "dp"),
        P("section", "dp", "tensor"),
        P("section", "tensor", "dp"),
        P("section", "dp"),
        P("section", "dp"),
    )
    return jax.shard_map(body, mesh=mesh, in_specs=in_specs, out_specs=out_specs, check_vma=False)
```

```python
import functools
import math

import jax
import jax.numpy as jnp
from jax import lax
from jax.experimental import pallas as pl
from jax.experimental.pallas import tpu as pltpu
from jax.sharding import PartitionSpec as P

MODEL_WIDTH = 8192
MESH = pl.DeviceIdType.MESH

epsilon = 1e-05
inv_root_two = 0.7071067811865476
inv_root_two_pi = 0.3989422804014327


def relay_kernel(kind, n, first, *refs):
    has_pre, has_act = kind != "grad", kind != "value"
    it = iter(refs)
    norm_ref = next(it) if has_pre else None
    inc_ref = next(it) if has_act else None
    slope_refs = (next(it), next(it)) if kind == "grad" else None
    up_hbm = next(it)
    down_hbm = next(it) if has_act else None
    act_ref = next(it) if has_pre else None
    slope_out = next(it) if kind == "value" else None
    pg_ref, ng_ref = (next(it), next(it)) if has_act else (None, None)
    up_v, up_sem = next(it), next(it)
    down_v, down_sem = (next(it), next(it)) if has_act else (None, None)
    own, right_sum, left_sum = next(it), next(it), next(it)
    send_r, recv_r, send_l, recv_l = next(it), next(it), next(it), next(it)
    acc = next(it) if has_act else None
    slope_v = next(it) if kind == "grad" else None

    chunks, width = up_v.shape[0], up_v.shape[2]
    streams, parts, rows = own.shape[0], own.shape[2], own.shape[3]
    me = lax.axis_index("dp")
    not_first, not_last = me > 0, me < n - 1

    def up_copy(c):
        cols = pl.ds(pl.multiple_of((first + c) * width, width), width)
        return pltpu.make_async_copy(up_hbm.at[:, cols], up_v.at[c], up_sem.at[c])

    def down_copy(c):
        slots = down_v.shape[0]
        span = pl.ds(pl.multiple_of(c * width, width), width)
        slot = lax.rem(c, slots)
        return pltpu.make_async_copy(down_hbm.at[span, :], down_v.at[slot], down_sem.at[slot])

    def right_copy(s, c, h):
        block = right_sum.at[s, c, h]
        return pltpu.make_async_remote_copy(
            block, block, send_r.at[s, c, h], recv_r.at[s, c, h],
            device_id={"dp": jnp.minimum(me + 1, n - 1)}, device_id_type=MESH)

    def left_copy(s, c, h):
        block = left_sum.at[s, c, h]
        return pltpu.make_async_remote_copy(
            block, block, send_l.at[s, c, h], recv_l.at[s, c, h],
            device_id={"dp": jnp.maximum(me - 1, 0)}, device_id_type=MESH)

    if has_act:
        for c in range(min(down_v.shape[0], chunks)):
            down_copy(c).start()
    lax.fori_loop(0, chunks, lambda c, _: (up_copy(c).start(), 0)[1], 0)

    barrier = pltpu.get_barrier_semaphore()

    @pl.when(not_first)
    def _():
        pl.semaphore_signal(barrier, inc=1, device_id={"dp": me - 1}, device_id_type=MESH)

    @pl.when(not_last)
    def _():
        pl.semaphore_signal(barrier, inc=1, device_id={"dp": me + 1}, device_id_type=MESH)

    pl.semaphore_wait(barrier, jnp.where(not_first, 1, 0) + jnp.where(not_last, 1, 0))

    if has_act:
        acc[...] = jnp.zeros_like(acc)

    def forward(s, c, h, arrives, leaves, buf, copy):
        @pl.when(arrives)
        def _():
            copy(s, c, h).wait_recv()
            buf[s, c, h] = (buf[s, c, h].astype(jnp.float32) + own[s, c, h].astype(jnp.float32)).astype(jnp.bfloat16)

        @pl.when(jnp.logical_not(arrives))
        def _():
            buf[s, c, h] = own[s, c, h]

        @pl.when(leaves)
        def _():
            copy(s, c, h).start()

    def whole(s, c):
        total = (right_sum[s, c].astype(jnp.float32) + left_sum[s, c].astype(jnp.float32)
                 - own[s, c].astype(jnp.float32))
        return total.reshape(parts * rows, width)

    def keep(s, c, product):
        own[s, c] = product.astype(jnp.bfloat16).reshape(parts, rows, width)

    def step(t, carry):
        @pl.when(t < chunks)
        def _():
            up_copy(t).wait()
            if has_pre:
                keep(0, t, jnp.dot(norm_ref[...], up_v[t], preferred_element_type=jnp.float32))
            if has_act:
                down_copy(t).wait()
                keep(streams - 1, t, lax.dot_general(
                    inc_ref[...], down_v[lax.rem(t, down_v.shape[0])], (((1,), (1,)), ((), ())),
                    preferred_element_type=jnp.float32))

                @pl.when(t + down_v.shape[0] < chunks)
                def _():
                    down_copy(t + down_v.shape[0]).start()

        cr = t - 2 * me
        cl = t - 2 * (n - 1 - me)
        for h in range(parts):
            for s in range(streams):
                @pl.when(jnp.logical_and(cr >= 0, cr < chunks))
                def _():
                    forward(s, cr, h, not_first, not_last, right_sum, right_copy)

                @pl.when(jnp.logical_and(cl >= 0, cl < chunks))
                def _():
                    forward(s, cl, h, not_last, not_first, left_sum, left_copy)

        c = t - 2 * (n - 1)
        @pl.when(c >= 0)
        def _():
            cols = pl.ds(pl.multiple_of(c * width, width), width)
            if has_pre:
                pre = whole(0, c)
                cdf = 0.5 * (1.0 + lax.erf(pre * inv_root_two))
                slope = cdf + pre * jnp.exp(-0.5 * pre * pre) * inv_root_two_pi
                act_ref[:, cols] = (pre * cdf).astype(jnp.bfloat16)
                if kind == "value":
                    slope_out[:, cols] = slope
            else:
                half = chunks // 2
                for side in range(2):
                    @pl.when(c // half == side)
                    def _():
                        part = pl.ds(pl.multiple_of((c - side * half) * width, width), width)
                        slope_v[...] = slope_refs[side][:, part]

                slope = slope_v[...]
            if has_act:
                grad = (whole(streams - 1, c) * slope).astype(jnp.bfloat16)
                pg_ref[:, cols] = grad
                acc[...] += lax.dot_general(grad, up_v[c], (((1,), (1,)), ((), ())),
                                            preferred_element_type=jnp.float32)
        return carry

    lax.fori_loop(0, chunks + 2 * (n - 1), step, 0)

    if has_act:
        ng_ref[...] = acc[...].astype(jnp.bfloat16)

    def drain(c, carry):
        for s in range(streams):
            for h in range(parts):
                @pl.when(not_last)
                def _():
                    right_copy(s, c, h).wait_send()

                @pl.when(not_first)
                def _():
                    left_copy(s, c, h).wait_send()
        return carry

    lax.fori_loop(0, chunks, drain, 0)


def relay(kind, collective_id, lhs, up, down=None, first=0, share=1):
    n = lax.axis_size("dp")
    tokens = lhs[0].shape[0]
    features, hidden = up.shape[0], up.shape[1] // share
    width, parts = 256, 2
    chunks = hidden // width
    has_pre, has_act = kind != "grad", kind != "value"
    streams = 2 if kind == "both" else 1
    vmem = pl.BlockSpec(memory_space=pltpu.VMEM)
    hbm = pl.BlockSpec(memory_space=pl.ANY)
    wide = jax.ShapeDtypeStruct((tokens, hidden), jnp.bfloat16)
    outs = []
    if has_pre:
        outs.append(wide)
    if kind == "value":
        outs.append(jax.ShapeDtypeStruct((tokens, hidden), jnp.float32))
    if has_act:
        outs += [wide, jax.ShapeDtypeStruct((tokens, features), jnp.bfloat16)]
    sems = pltpu.SemaphoreType.DMA
    scratch = [pltpu.VMEM((chunks, features, width), jnp.bfloat16), sems((chunks,))]
    if has_act:
        scratch += [pltpu.VMEM((4, width, features), jnp.bfloat16), sems((4,))]
    scratch += [pltpu.VMEM((streams, chunks, parts, tokens // parts, width), jnp.bfloat16)] * 3
    scratch += [sems((streams, chunks, parts))] * 4
    if has_act:
        scratch.append(pltpu.VMEM((tokens, features), jnp.float32))
    if kind == "grad":
        scratch.append(pltpu.VMEM((tokens, width), jnp.float32))
    weights = [up] + ([down] if has_act else [])
    products = (1 if has_pre else 0) + (2 if has_act else 0)
    return pl.pallas_call(
        functools.partial(relay_kernel, kind, n, first * (hidden // width)),
        out_shape=outs,
        in_specs=[vmem] * len(lhs) + [hbm] * len(weights),
        out_specs=[vmem] * len(outs),
        scratch_shapes=scratch,
        compiler_params=pltpu.CompilerParams(
            collective_id=collective_id, has_side_effects=True,
            vmem_limit_bytes=52 * 1024 * 1024),
        cost_estimate=pl.CostEstimate(
            flops=2 * tokens * features * hidden * products,
            bytes_accessed=streams * 160 * 1024 * 1024 // share, transcendentals=0),
        name="relay_%s_%d" % (kind, first),
    )(*lhs, *weights)


def scatter_rows(partial_gradient):
    return lax.psum_scatter(partial_gradient, "tensor", scatter_dimension=0, tiled=True)


def finish(scattered, centered_input, inverse_deviation, scale_gain, local_rows):
    normalized_gradient = scattered.astype(jnp.float32)
    gain_product = jnp.sum(normalized_gradient * centered_input, axis=0)
    bias_term = jnp.sum(normalized_gradient, axis=0)
    centered_gradient = normalized_gradient * scale_gain
    centered_total, centered_cross = lax.psum(
        (
            jnp.sum(centered_gradient, axis=1, keepdims=True),
            jnp.sum(centered_gradient * centered_input, axis=1, keepdims=True),
        ),
        "dp",
    )
    final_output = local_rows.astype(jnp.float32) + inverse_deviation * (
        centered_gradient
        - centered_total / MODEL_WIDTH
        - centered_input * (centered_cross / MODEL_WIDTH)
    )
    return final_output.astype(jnp.bfloat16), gain_product, bias_term


def gather_rows(block):
    return lax.all_gather(block, "tensor", axis=0, tiled=True)


def body(layer_input, ready_grad, late_grad, norm_gain, norm_bias, up_weight, down_weight):
    early = lax.axis_index("section") == 0
    scale_gain = norm_gain[0]
    shift_bias = norm_bias[0]
    weight_up = up_weight[0]
    weight_down = down_weight[0]
    ready_whole = gather_rows(ready_grad[0])
    inputs_float = layer_input[0].astype(jnp.float32)
    row_total, row_squares = lax.psum(
        (
            jnp.sum(inputs_float, axis=2, keepdims=True),
            jnp.sum(inputs_float * inputs_float, axis=2, keepdims=True),
        ),
        "dp",
    )
    row_mean = row_total / MODEL_WIDTH
    variance = row_squares / MODEL_WIDTH - row_mean * row_mean
    inverse_deviation = lax.rsqrt(variance + epsilon)
    centered_input = (inputs_float - row_mean) * inverse_deviation
    normalized = (centered_input * scale_gain + shift_bias).astype(jnp.bfloat16)
    normed_first = gather_rows(normalized[0])
    act_first, pre_grad_first, partial_first = relay(
        "both", 1, [normed_first, ready_whole], weight_up, weight_down)
    normed_second = gather_rows(normalized[1])
    normed_second, partial_first = lax.optimization_barrier((normed_second, partial_first))
    scattered = scatter_rows(partial_first)
    act_low, slope_low = relay("value", 2, [normed_second], weight_up, first=0, share=2)
    scattered, act_low = lax.optimization_barrier((scattered, act_low))
    first_out, first_gain, first_bias = finish(
        scattered, centered_input[0], inverse_deviation[0], scale_gain, ready_grad[0])

    arrived = lax.ppermute(first_out, "section", [(1, 0)])
    second_rows = jnp.where(early, arrived, late_grad)
    second_rows, normed_second = lax.optimization_barrier((second_rows, normed_second))
    second_incoming = gather_rows(second_rows)
    act_high, slope_high = relay("value", 4, [normed_second], weight_up, first=1, share=2)
    act_second = jnp.concatenate([act_low, act_high], axis=1)
    pre_grad_second, partial_second = relay(
        "grad", 3, [second_incoming, slope_low, slope_high], weight_up, weight_down)
    second_out, second_gain, second_bias = finish(
        scatter_rows(partial_second), centered_input[1], inverse_deviation[1], scale_gain, second_rows)

    scale = 1.0 / math.sqrt(2 * second_incoming.shape[0])

    def weight_grad(left, right):
        return (lax.dot_general(
            jnp.concatenate(left), jnp.concatenate(right), (((0,), (0,)), ((), ())),
            preferred_element_type=jnp.float32) * scale).astype(jnp.bfloat16)

    down_part = weight_grad([act_first, act_second], [ready_whole, second_incoming])
    up_part = weight_grad([normed_first, normed_second], [pre_grad_first, pre_grad_second])
    token_sums = jnp.stack([first_gain + second_gain, first_bias + second_bias])
    gain_sum, bias_sum = jnp.sum(lax.all_gather(token_sums, "tensor", axis=0), axis=0)
    results = jnp.stack([first_out, second_out])
    return (
        results[None],
        up_part[None],
        down_part[None],
        (gain_sum * scale)[None],
        (bias_sum * scale)[None],
    )


def solution(mesh):
    in_specs = (
        P("section", None, "tensor", "dp"),
        P("section", "tensor", "dp"),
        P("tensor", "dp"),
        P("section", "dp"),
        P("section", "dp"),
        P("section", "dp", "tensor"),
        P("section", "tensor", "dp"),
    )
    out_specs = (
        P("section", None, "tensor", "dp"),
        P("section", "dp", "tensor"),
        P("section", "tensor", "dp"),
        P("section", "dp"),
        P("section", "dp"),
    )
    return jax.shard_map(body, mesh=mesh, in_specs=in_specs, out_specs=out_specs, check_vma=False)
```
